32 devices in a mesh: node: 8 (over z, y), local: 4 (over x, core).
Axes of the slice: x: 2, y: 2, z: 4, core: 2. Of those that a mesh axis runs over, the one named last changes fastest.
Arguments:
- tokens: bfloat16 [1024, 4096], P(('node', 'local')), may hold values from -6 to 6
- out_grad: bfloat16 [1024, 4096], P(('node', 'local')), may hold values from -6 to 6
- node_lists: int32 [1024, 4], P(('node', 'local')), may hold values from 0 to 7, as said below
- expert_local: int32 [1024, 8], P(('node', 'local')), may hold values from 0 to 15, as said below
- gate_fixed: int32 [1024, 8], P(('node', 'local')), may hold values from 4096 to 65535
- gate_weight: bfloat16 [32, 4096, 768], P(('node', 'local')), may hold values from -0.09375 to 0.09375
- up_weight: bfloat16 [32, 4096, 768], P(('node', 'local')), may hold values from -0.09375 to 0.09375
- down_weight: bfloat16 [32, 768, 4096], P(('node', 'local')), may hold values from -0.21875 to 0.21875
Outputs:
- token_grad: bfloat16 [1024, 4096], P(('node', 'local'))
- down_grad: bfloat16 [32, 768, 4096], P(('node', 'local'))
The draws below stay inside these ranges and needn't reach their ends.
Inputs may be any that keep to these rules, and one draw needn't show every extreme that they name: `node_lists`: each row holds 4 different group numbers. `expert_local`: each row holds 8 different numbers.
All inputs are finite; a program needn't handle non-finite values.
Results may differ from the reference program's by a relative error of at most 0.0064.
Values may be sent and summed in bfloat16 or wider, within the bound.
No kernel may reach another device: no remote copies, remote signals or barrier semaphores. Data moves between devices by JAX's collectives and lax.ppermute only.
A program may use at most 128 MiB of HBM per device.

```python
import jax
import jax.numpy as jnp
from jax import lax

D = 4096
TOP = 8
FWIN = 768
NODE_LIM = 4
TOK_DEV = 32
NODES = 8
PER_NODE = 4
EXPERTS = 32
TOKENS = 1024
CAP = 8


def routing_pair(key):
    base = jax.random.fold_in(key, 11)
    subkeys = jax.random.split(base, 5)
    node_bias = jax.random.randint(subkeys[0], (NODES,), 0, 3 * 4096)
    node_noise = jax.random.randint(subkeys[1], (TOKENS, NODES), 0, 4 * 4096)
    hot_node = jax.random.randint(subkeys[2], (EXPERTS,), 0, NODES)
    hot_local = jax.random.randint(subkeys[3], (EXPERTS,), 0, PER_NODE)
    token_pos = jnp.arange(TOKENS, dtype=jnp.int32)
    block_of = token_pos // TOK_DEV
    forced = token_pos % TOK_DEV < CAP
    node_iota = jnp.arange(NODES, dtype=jnp.int32)[None, :]
    boost_node = jnp.where(forced[:, None] & (node_iota == hot_node[block_of][:, None]), 100000, 0)
    node_score = (node_noise + node_bias[None, :] + boost_node) * NODES + node_iota
    _, node_lists = lax.top_k(node_score, NODE_LIM)
    width_pick = NODE_LIM * PER_NODE
    pick_noise = jax.random.randint(subkeys[4], (TOKENS, width_pick), 0, 4096)
    pick_iota = jnp.arange(width_pick, dtype=jnp.int32)[None, :]
    boost_pick = jnp.where(forced[:, None] & (pick_iota == hot_local[block_of][:, None]), 100000, 0)
    pick_score = (pick_noise + boost_pick) * width_pick + pick_iota
    _, expert_local = lax.top_k(pick_score, TOP)
    return (node_lists.astype(jnp.int32), expert_local.astype(jnp.int32))


def draw_node_lists(key, part):
    return routing_pair(key)[0]


def draw_expert_local(key, part):
    return routing_pair(key)[1]


def with_ends(values, own_key, smallest, largest):
    index_at = [jax.random.randint(jax.random.fold_in(own_key, axis), (), 0, length) for axis, length in enumerate(values.shape)]
    widest = values.shape.index(max(values.shape))
    neighbour = index_at[:widest] + [(index_at[widest] + 1) % values.shape[widest]] + index_at[widest + 1:]
    return values.at[tuple(index_at)].set(smallest).at[tuple(neighbour)].set(largest)


def shard_levels(key, dims, cuts, low, top_value):
    level, own = 1.0, jax.random.fold_in(key, 6)
    for dim, shards_of in cuts:
        steps = jnp.exp(jax.random.uniform(jax.random.fold_in(own, dim), (shards_of,), jnp.float32, low / len(cuts), top_value / len(cuts)))
        level = level * jnp.repeat(steps, dims[dim] // shards_of).reshape([-1 if axis == dim else 1 for axis in range(len(dims))])
    return level


def gaussian(key, extent, scale, most, pieces=(), kind=jnp.bfloat16):
    level = shard_levels(key, extent, pieces, -0.22, 0.18) if pieces else 1.0
    array = jax.random.normal(key, extent, jnp.float32) * scale * level
    return jnp.minimum(jnp.maximum(array, -most), most).astype(kind)


def setup_inputs(seed: int = 0) -> dict:
    arg_keys = jax.random.split(jax.random.key(seed), 9)
    return {
        "tokens": gaussian(arg_keys[0], (TOKENS, D), 1.0, 6.0, ((0, 32),)),
        "out_grad": gaussian(arg_keys[1], (TOKENS, D), 1.0, 6.0, ((0, 32),)),
        "node_lists": draw_node_lists(jax.random.fold_in(arg_keys[8], 71), 0),
        "expert_local": draw_expert_local(jax.random.fold_in(arg_keys[8], 71), 0),
        "gate_fixed": with_ends(jax.random.randint(arg_keys[4], (TOKENS, TOP), 4096, 65536), jax.random.fold_in(arg_keys[4], 1), 4096, 65535).astype(jnp.int32),
        "gate_weight": gaussian(arg_keys[5], (EXPERTS, D, FWIN), D ** -0.5, 0.09375, ((0, 32),)),
        "up_weight": gaussian(arg_keys[6], (EXPERTS, D, FWIN), D ** -0.5, 0.09375, ((0, 32),)),
        "down_weight": gaussian(arg_keys[7], (EXPERTS, FWIN, D), FWIN ** -0.5, 0.21875, ((0, 32),)),
    }


def route_table(node_lists, expert_local):
    node_pick = jnp.take_along_axis(node_lists, (expert_local // PER_NODE).astype(jnp.int32), axis=1)
    expert_ids = (node_pick * PER_NODE + expert_local % PER_NODE).astype(jnp.int32)
    block_ids = expert_ids.reshape(EXPERTS, TOK_DEV * TOP)
    onehot = (block_ids[:, :, None] == jnp.arange(EXPERTS, dtype=jnp.int32)[None, None, :]).astype(jnp.int32)
    running = jnp.cumsum(onehot, axis=1)
    slot = jnp.sum(onehot * running, axis=2) - 1
    kept = slot < CAP
    source = jnp.arange(EXPERTS, dtype=jnp.int32)[:, None]
    position = jnp.where(kept, (block_ids * EXPERTS + source) * CAP + slot, EXPERTS * EXPERTS * CAP).astype(jnp.int32)
    assign_index = (source * (TOK_DEV * TOP) + jnp.arange(TOK_DEV * TOP, dtype=jnp.int32)[None, :]).astype(jnp.int32)
    table = jnp.full((EXPERTS * EXPERTS * CAP,), -1, jnp.int32)
    table = table.at[position.reshape(-1)].set(assign_index.reshape(-1), mode="drop")
    return table.reshape(EXPERTS, EXPERTS * CAP)


def reference(tokens, out_grad, node_lists, expert_local, gate_fixed, gate_weight, up_weight, down_weight):
    table = route_table(node_lists, expert_local)
    gate_flat = gate_fixed.reshape(-1)

    def one_expert(carry, inputs):
        assign, w_gate_e, w_up_e, w_down_e = inputs
        valid = assign >= 0
        safe = jnp.maximum(assign, 0).astype(jnp.int32)
        rows = (safe // TOP).astype(jnp.int32)
        x_rows = jnp.where(valid[:, None], tokens[rows], jnp.zeros((), jnp.bfloat16)).astype(jnp.bfloat16)
        gate_val = gate_flat[safe].astype(jnp.float32) * (1.0 / 65536.0)
        dy_rows = jnp.where(valid[:, None], gate_val[:, None] * out_grad[rows].astype(jnp.float32), jnp.float32(0.0)).astype(jnp.bfloat16)
        gate_act = jnp.dot(x_rows, w_gate_e, preferred_element_type=jnp.float32)
        up_act = jnp.dot(x_rows, w_up_e, preferred_element_type=jnp.float32)
        sig = jax.nn.sigmoid(gate_act)
        hidden = (gate_act * sig * up_act).astype(jnp.bfloat16)
        down_g = lax.dot_general(hidden, dy_rows, (((0,), (0,)), ((), ())), preferred_element_type=jnp.float32).astype(jnp.bfloat16)
        hidden_grad = jnp.dot(dy_rows, w_down_e.T, preferred_element_type=jnp.float32)
        gate_grad = (hidden_grad * up_act * sig * (1.0 + gate_act * (1.0 - sig))).astype(jnp.bfloat16)
        up_grad = (hidden_grad * gate_act * sig).astype(jnp.bfloat16)
        row_grad = (jnp.dot(gate_grad, w_gate_e.T, preferred_element_type=jnp.float32)
                    + jnp.dot(up_grad, w_up_e.T, preferred_element_type=jnp.float32)).astype(jnp.bfloat16)
        row_grad = lax.optimization_barrier(row_grad)
        added = jnp.where(valid[:, None], row_grad.astype(jnp.float32), jnp.float32(0.0))
        carry = carry.at[rows].add(added)
        return carry, down_g

    start = jnp.zeros((TOKENS, D), jnp.float32)
    total, down_grad = lax.scan(one_expert, start, (table, gate_weight, up_weight, down_weight))
    return total.astype(jnp.bfloat16), down_grad
```

```python
import jax
import jax.numpy as jnp
from jax import lax
from jax.sharding import PartitionSpec as P

AXES = ("node", "local")
BF16 = jnp.bfloat16
F32 = jnp.float32


def device_perms(nodes, per_node):
    depth = nodes // 2
    order = [z for z in range(depth) if z == 0 or z % 2 == 1]
    order += [z for z in reversed(range(depth)) if z not in order]
    follow = {order[i]: order[(i + 1) % depth] for i in range(depth)}

    def flat(z, y, place):
        return (z * 2 + y) * per_node + place

    cells = [(z, y, p) for z in range(depth) for y in range(2) for p in range(per_node)]
    ring = [(flat(z, y, p), flat(follow[z], y, p)) for z, y, p in cells]
    back = [(b, a) for a, b in ring]
    flip_x = [(flat(z, y, p), flat(z, y, p ^ 2)) for z, y, p in cells]
    flip_y = [(flat(z, y, p), flat(z, 1 - y, p)) for z, y, p in cells]
    flip_xy = [(flat(z, y, p), flat(z, 1 - y, p ^ 2)) for z, y, p in cells]
    flip_core = [(flat(z, y, p), flat(z, y, p ^ 1)) for z, y, p in cells]
    return depth, ring, back, (flip_x, flip_y, flip_xy), flip_core


def route(node_lists, expert_local, gate_fixed, experts, per_node, capacity):
    tok_dev = expert_local.shape[0]
    place = expert_local // per_node
    group = jnp.zeros_like(expert_local)
    for j in range(node_lists.shape[1]):
        group = jnp.where(place == j, node_lists[:, j : j + 1], group)
    expert = group * per_node + expert_local % per_node
    ids = jnp.arange(experts, dtype=jnp.int32)
    member = jnp.any(expert[:, :, None] == ids[None, None, :], axis=1)
    earlier = jnp.tril(jnp.ones((tok_dev, tok_dev), BF16), -1)
    before = jnp.dot(earlier, member.astype(BF16), preferred_element_type=F32).astype(jnp.int32)
    slot = jnp.sum(jnp.where(expert[:, :, None] == ids[None, None, :], before[:, None, :], 0), axis=2)
    code = jnp.where(slot < capacity, expert * capacity + slot, -1)
    meta = jnp.concatenate([code, gate_fixed // 256, gate_fixed % 256], axis=1).astype(BF16)
    return jnp.pad(meta, ((0, 0), (0, -meta.shape[1] % 128)))


def selection(meta, top, codes):
    meta = meta.astype(F32)
    code = meta[:, :top].astype(jnp.int32)
    gate = meta[:, top : 2 * top] * 256.0 + meta[:, 2 * top : 3 * top]
    hit = code[:, :, None] == codes[None, None, :]
    pick = jnp.any(hit, axis=1)
    gate = jnp.sum(jnp.where(hit, gate[:, :, None], 0.0), axis=(0, 1))
    return pick.astype(BF16), gate


def expert_math(x_rows, dy_rows, w_gate_e, w_up_e, w_down_e):
    gate_act = jnp.dot(x_rows, w_gate_e, preferred_element_type=F32)
    up_act = jnp.dot(x_rows, w_up_e, preferred_element_type=F32)
    sig = jax.nn.sigmoid(gate_act)
    hidden = (gate_act * sig * up_act).astype(BF16)
    rows = (((0,), (0,)), ((), ()))
    last = (((1,), (1,)), ((), ()))
    down_local = lax.dot_general(hidden, dy_rows, rows, preferred_element_type=F32).astype(BF16)
    hidden_grad = lax.dot_general(dy_rows, w_down_e, last, preferred_element_type=F32)
    gate_grad = (hidden_grad * up_act * sig * (1.0 + gate_act * (1.0 - sig))).astype(BF16)
    up_grad = (hidden_grad * gate_act * sig).astype(BF16)
    row_grad = (
        lax.dot_general(gate_grad, w_gate_e, last, preferred_element_type=F32)
        + lax.dot_general(up_grad, w_up_e, last, preferred_element_type=F32)
    ).astype(BF16)
    return down_local, row_grad


def body(
    tokens, out_grad, node_lists, expert_local, gate_fixed, gate_weight, up_weight, down_weight
):
    nodes, per_node = lax.axis_size("node"), lax.axis_size("local")
    experts = nodes * per_node
    tok_dev, top = expert_local.shape
    width = tokens.shape[1]
    capacity = tok_dev * top // experts
    depth, ring, back, flips, flip_core = device_perms(nodes, per_node)
    places = per_node // 2

    node, place = lax.axis_index("node"), lax.axis_index("local")
    plane = node // 2 * 2 * per_node
    here = (node % 2) * per_node + place
    chips = (0, 2, per_node, per_node + 2)
    reach = jnp.array([a ^ b for a in chips for b in (0, 1)], jnp.int32)
    slots = jnp.arange(capacity, dtype=jnp.int32)
    codes = ((plane + (here ^ reach))[:, None] * capacity + slots[None, :]).reshape(-1)
    pair = 2 * capacity

    meta = route(node_lists, expert_local, gate_fixed, experts, per_node, capacity)
    held = jnp.concatenate([tokens, out_grad, meta], axis=1)
    first = jnp.arange(2 * width)[None, :] < width
    picks, mine, other = [], [], []
    for step in range(depth):
        coming = lax.ppermute(held, AXES, ring) if step < depth - 1 else None
        pick, gate = selection(held[:, 2 * width :], top, codes)
        picks.append(pick)
        chosen = lax.dot_general(
            pick, held[:, : 2 * width], (((0,), (0,)), ((), ())), preferred_element_type=F32
        )
        scale = jnp.where(first, 1.0, (gate * (1.0 / 65536.0))[:, None])
        chosen = (chosen * scale).astype(BF16)
        got = [chosen[:pair]]
        for i, flip in enumerate(flips):
            got.append(lax.ppermute(chosen[(i + 1) * pair : (i + 2) * pair], AXES, flip))
        mine += [g[:capacity] for g in got]
        other += [g[capacity:] for g in got]
        held = coming
    cut = 4 * (depth - 1)
    crossed = [lax.ppermute(jnp.concatenate(part, axis=0), AXES, flip_core) for part in (other[:cut], other[cut:])]
    rows = jnp.concatenate(mine + crossed, axis=0)

    down_local, row_grad = expert_math(
        rows[:, :width], rows[:, width:], gate_weight[0], up_weight[0], down_weight[0]
    )

    half = depth * 4 * capacity
    own = row_grad[:half].reshape(depth, 4, capacity, width)
    theirs = row_grad[half:].reshape(depth, 4, capacity, width)
    last = lax.ppermute(theirs[depth - 1 :], AXES, flip_core)
    rest = lax.ppermute(theirs[: depth - 1], AXES, flip_core)
    total = None
    for step in reversed(range(depth)):
        swapped = last[0] if step == depth - 1 else rest[step]
        both = jnp.concatenate([own[step], swapped], axis=1)
        got = [both[0]] + [lax.ppermute(both[i + 1], AXES, flip) for i, flip in enumerate(flips)]
        partial = jnp.dot(picks[step], jnp.concatenate(got, axis=0), preferred_element_type=F32)
        if total is not None:
            partial = partial + total.astype(F32)
        total = partial.astype(BF16)
        if step:
            total = lax.ppermute(total, AXES, back)
    return total, down_local[None]


def solution(mesh):
    split = P(AXES)
    return jax.shard_map(
        body, mesh=mesh, in_specs=(split,) * 8, out_specs=(split, split), check_vma=False
    )
```

```python
import functools

import jax
import jax.numpy as jnp
from jax import lax
from jax.experimental import pallas as pl
from jax.experimental.pallas import tpu as pltpu
from jax.sharding import PartitionSpec as P

AXES = ("node", "local")
BF16 = jnp.bfloat16
F32 = jnp.float32
COLUMNS = 1024
META = 128
NEAR = 2


def device_perms(nodes, per_node):
    depth = nodes // 2
    order = [z for z in range(depth) if z == 0 or z % 2 == 1]
    order += [z for z in reversed(range(depth)) if z not in order]
    follow = {order[i]: order[(i + 1) % depth] for i in range(depth)}

    def flat(z, y, place):
        return (z * 2 + y) * per_node + place

    cells = [(z, y, p) for z in range(depth) for y in range(2) for p in range(per_node)]
    ring = [(flat(z, y, p), flat(follow[z], y, p)) for z, y, p in cells]
    back = [(b, a) for a, b in ring]
    flip_x = [(flat(z, y, p), flat(z, y, p ^ 2)) for z, y, p in cells]
    flip_y = [(flat(z, y, p), flat(z, 1 - y, p)) for z, y, p in cells]
    flip_xy = [(flat(z, y, p), flat(z, 1 - y, p ^ 2)) for z, y, p in cells]
    flip_core = [(flat(z, y, p), flat(z, y, p ^ 1)) for z, y, p in cells]
    return depth, ring, back, (flip_x, flip_y, flip_xy), flip_core


def slot_codes(spot, per_node, capacity):
    rank = lax.broadcasted_iota(jnp.int32, (8 * capacity, 1), 0)
    flip, slot = rank // capacity, rank % capacity
    reach = flip // 4 * per_node + flip % 4
    return ((spot[0] + (spot[1] ^ reach)) * capacity + slot).astype(F32)


def pick_rows(meta, codes, tok, grad, top, outs, pick_ref):
    tok_dev, width = tok.shape
    hit = None
    gate = jnp.zeros(codes.shape, F32)
    for k in range(top):
        same = meta[k : k + 1, :tok_dev] == codes
        value = meta[top + k : top + k + 1, :tok_dev] * 256.0 + meta[2 * top + k : 2 * top + k + 1, :tok_dev]
        gate = gate + jnp.sum(jnp.where(same, value, 0.0), axis=1, keepdims=True)
        hit = same if hit is None else hit | same
    pick = jnp.where(hit, 1.0, 0.0).astype(BF16)
    pick_ref[...] = pick
    scale = gate * (1.0 / 65536.0)
    pair = codes.shape[0] // 4
    for c in range(0, width, COLUMNS):
        cols = slice(c, min(c + COLUMNS, width))
        x = jnp.dot(pick, tok[:, cols], preferred_element_type=F32).astype(BF16)
        dy = (jnp.dot(pick, grad[:, cols], preferred_element_type=F32) * scale).astype(BF16)
        for i, (out_x, out_dy) in enumerate(outs):
            out_x[:, cols] = x[i * pair : (i + 1) * pair]
            out_dy[:, cols] = dy[i * pair : (i + 1) * pair]


def first_kernel(per_node, capacity, experts, spot, *refs):
    far, (*outs, pick_ref, held, codes_ref) = refs[:5], refs[5:12]
    (lists, local, gate, tok, grad), meta, sems = refs[12:17], refs[17], refs[18]
    copies = [pltpu.make_async_copy(a, b, sems.at[i]) for i, (a, b) in enumerate(zip(far, refs[12:17]))]
    for copy in copies:
        copy.start()
    for copy in copies[:3]:
        copy.wait()
    top, tok_dev = local.shape
    width = tok.shape[1]
    place = local[...] // per_node
    group = jnp.zeros_like(place)
    for j in range(lists.shape[0]):
        group = jnp.where(place == j, lists[j : j + 1, :], group)
    expert = group * per_node + local[...] % per_node
    ids = lax.broadcasted_iota(jnp.int32, (experts, tok_dev), 0)
    member = None
    for k in range(top):
        same = ids == expert[k : k + 1, :]
        member = same if member is None else member | same
    rows = lax.broadcasted_iota(jnp.int32, (tok_dev, tok_dev), 0)
    cols = lax.broadcasted_iota(jnp.int32, (tok_dev, tok_dev), 1)
    earlier = jnp.where(rows < cols, 1.0, 0.0).astype(BF16)
    before = jnp.dot(jnp.where(member, 1.0, 0.0).astype(BF16), earlier, preferred_element_type=F32)
    meta[...] = jnp.zeros(meta.shape, F32)
    for k in range(top):
        slot = jnp.sum(jnp.where(ids == expert[k : k + 1, :], before, 0.0), axis=0, keepdims=True)
        code = expert[k : k + 1, :].astype(F32) * capacity + slot
        meta[k : k + 1, :tok_dev] = jnp.where(slot < capacity, code, -1.0)
    meta[top : 2 * top, :tok_dev] = (gate[...] // 256).astype(F32)
    meta[2 * top : 3 * top, :tok_dev] = (gate[...] % 256).astype(F32)
    for copy in copies[3:]:
        copy.wait()
    held[:, :width] = tok[...]
    held[:, width : 2 * width] = grad[...]
    held[:, 2 * width :] = meta[...].astype(BF16)
    codes = slot_codes(spot, per_node, capacity)
    codes_ref[...] = codes
    pick_rows(meta, codes, tok, grad, top, [(out.at[0], out.at[1]) for out in outs], pick_ref)


def next_kernel(top, codes, held, *refs):
    *outs, pick_ref = refs
    width = outs[0].shape[-1]
    meta = held[:, 2 * width :].astype(F32)
    tok, grad = held.at[:, :width], held.at[:, width : 2 * width]
    pairs = list(zip(outs[:4], outs[4:])) if len(outs) == 8 else [(out.at[0], out.at[1]) for out in outs]
    pick_rows(meta, codes[...], tok, grad, top, pairs, pick_ref)


def whole(n):
    return [pl.BlockSpec(memory_space=pltpu.VMEM)] * n


def row_shapes(capacity, tok_dev, width, apart=False):
    shape = (2 * capacity, width)
    rows = [jax.ShapeDtypeStruct(shape, BF16)] * 8 if apart else [jax.ShapeDtypeStruct((2,) + shape, BF16)] * 4
    return rows + [jax.ShapeDtypeStruct((8 * capacity, tok_dev), BF16)]


PARAMS = pltpu.CompilerParams(vmem_limit_bytes=12 * 1024 * 1024)


def first_rows(per_node, capacity, experts, spot, lists, local, gate, tok, grad):
    shape = (tok.shape[0], 2 * tok.shape[1] + META)
    operands = [pltpu.with_memory_space_constraint(a, pltpu.HBM) for a in (lists, local, gate, tok, grad)]
    extra = [jax.ShapeDtypeStruct(shape, BF16), jax.ShapeDtypeStruct((8 * capacity, 1), F32)]
    return pl.pallas_call(
        functools.partial(first_kernel, per_node, capacity, experts),
        in_specs=[pl.BlockSpec(memory_space=pltpu.SMEM)] + [pl.BlockSpec(memory_space=pltpu.HBM)] * 5,
        out_specs=whole(7),
        out_shape=row_shapes(capacity, *tok.shape) + extra,
        scratch_shapes=[pltpu.VMEM(a.shape, a.dtype) for a in (lists, local, gate, tok, grad)]
        + [pltpu.VMEM((tok.shape[0], META), F32), pltpu.SemaphoreType.DMA((5,))],
        compiler_params=PARAMS,
        name="first_rows",
    )(spot, *operands)


def next_rows(top, codes, held, apart):
    shapes = row_shapes(codes.shape[0] // 8, held.shape[0], (held.shape[1] - META) // 2, apart)
    return pl.pallas_call(
        functools.partial(next_kernel, top),
        in_specs=whole(2),
        out_specs=whole(len(shapes)),
        out_shape=shapes,
        compiler_params=PARAMS,
        name="next_rows",
    )(codes, held)


def products(x_rows, w_gate_e, w_up_e):
    gate_act = jnp.dot(x_rows, w_gate_e, preferred_element_type=F32)
    up_act = jnp.dot(x_rows, w_up_e, preferred_element_type=F32)
    return gate_act, up_act


def gradients(gate_act, up_act, dy_rows, w_gate_e, w_up_e, w_down_e):
    last = (((1,), (1,)), ((), ()))
    sig = jax.nn.sigmoid(gate_act)
    hidden = (gate_act * sig * up_act).astype(BF16)
    hidden_grad = lax.dot_general(dy_rows, w_down_e, last, preferred_element_type=F32)
    gate_grad = (hidden_grad * up_act * sig * (1.0 + gate_act * (1.0 - sig))).astype(BF16)
    up_grad = (hidden_grad * gate_act * sig).astype(BF16)
    row_grad = (
        lax.dot_general(gate_grad, w_gate_e, last, preferred_element_type=F32)
        + lax.dot_general(up_grad, w_up_e, last, preferred_element_type=F32)
    ).astype(BF16)
    return hidden, row_grad


def ordered(held, got, w):
    near, far = got[w - 1][1:NEAR], got[w - 2][NEAR:] if w > 1 else []
    held, near, far = lax.optimization_barrier((held, near, far))
    got[w - 1][1:NEAR] = near
    if far:
        got[w - 2][NEAR:] = far
    return held


def body(
    tokens, out_grad, node_lists, expert_local, gate_fixed, gate_weight, up_weight, down_weight
):
    nodes, per_node = lax.axis_size("node"), lax.axis_size("local")
    experts = nodes * per_node
    tok_dev, top = expert_local.shape
    width = tokens.shape[1]
    capacity = tok_dev * top // experts
    depth, ring, back, flips, flip_core = device_perms(nodes, per_node)

    node, place = lax.axis_index("node"), lax.axis_index("local")
    spot = jnp.stack([node // 2 * 2 * per_node, (node % 2) * per_node + place])

    picks, got = [], []
    for w in range(depth - 1):
        if w == 0:
            *chosen, pick, held, codes = first_rows(
                per_node, capacity, experts, spot, node_lists.T, expert_local.T, gate_fixed.T, tokens, out_grad
            )
        else:
            ready = ordered(held, got, w)
            held = ready
            *chosen, pick = next_rows(top, codes, ready, False)
        picks.append(pick)
        got.append([chosen[0]] + [lax.ppermute(c, AXES, flip) for c, flip in zip(chosen[1:], flips)])
        held = lax.ppermute(held, AXES, ring)
    *chosen, pick = next_rows(top, codes, ordered(held, got, depth - 1), True)
    picks.append(pick)
    ends = []
    for part in (chosen[:4], chosen[4:]):
        ends.append([part[0]] + [lax.ppermute(c, AXES, flip) for c, flip in zip(part[1:], flips)])
    most = lax.ppermute(jnp.concatenate([g[:, capacity:] for window in got for g in window], axis=1), AXES, flip_core)

    def gather(i, end):
        rest = lax.ppermute(jnp.concatenate([g[capacity:] for g in end], axis=0), AXES, flip_core)
        own = [g[i, :capacity] for window in got for g in window] + [g[:capacity] for g in end]
        return jnp.concatenate(own + [most[i], rest], axis=0)

    x_rows = gather(0, ends[0])
    gate_act, up_act = products(x_rows, gate_weight[0], up_weight[0])
    gate_act, up_act, ends[1] = lax.optimization_barrier((gate_act, up_act, ends[1]))
    dy_rows = gather(1, ends[1])
    hidden, row_grad = gradients(gate_act, up_act, dy_rows, gate_weight[0], up_weight[0], down_weight[0])

    half = depth * 4 * capacity
    own = row_grad[:half].reshape(depth, 4, capacity, width)
    theirs = row_grad[half:].reshape(depth, 4, capacity, width)
    last = lax.ppermute(theirs[depth - 1], AXES, flip_core)
    rest = lax.ppermute(theirs[: depth - 1], AXES, flip_core)
    came = {}
    for w in reversed(range(depth)):
        both = jnp.concatenate([own[w], last if w == depth - 1 else rest[w]], axis=1)
        came[w] = [both[0]] + [lax.ppermute(both[i + 1], AXES, flip) for i, flip in enumerate(flips)]
    down_local = None
    total = None
    for w in reversed(range(depth)):
        partial = lax.dot_general(
            picks[w], jnp.concatenate(came[w], axis=0), (((0,), (0,)), ((), ())), preferred_element_type=F32
        )
        if total is not None:
            partial = partial + total.astype(F32)
        total = partial.astype(BF16)
        if w == 2:
            total, hidden = lax.optimization_barrier((total, hidden))
            down_local = lax.dot_general(
                hidden, dy_rows, (((0,), (0,)), ((), ())), preferred_element_type=F32
            ).astype(BF16)
        if w:
            if w == 1:
                total, down_local = lax.optimization_barrier((total, down_local))
            if w == 1:
                total, came[w - 1][1:2] = lax.optimization_barrier((total, came[w - 1][1:2]))
            total = lax.ppermute(total, AXES, back)
    return total, down_local[None]


def solution(mesh):
    split = P(AXES)
    return jax.shard_map(
        body, mesh=mesh, in_specs=(split,) * 8, out_specs=(split, split), check_vma=False
    )
```

```python
import functools

import jax
import jax.numpy as jnp
from jax import lax
from jax.experimental import pallas as pl
from jax.experimental.pallas import tpu as pltpu
from jax.sharding import PartitionSpec as P

AXES = ("node", "local")
BF16 = jnp.bfloat16
F32 = jnp.float32
COLUMNS = 1024
META = 128
NEAR = 2


def device_perms(nodes, per_node):
    depth = nodes // 2
    order = [z for z in range(depth) if z == 0 or z % 2 == 1]
    order += [z for z in reversed(range(depth)) if z not in order]
    follow = {order[i]: order[(i + 1) % depth] for i in range(depth)}

    def flat(z, y, place):
        return (z * 2 + y) * per_node + place

    cells = [(z, y, p) for z in range(depth) for y in range(2) for p in range(per_node)]
    ring = [(flat(z, y, p), flat(follow[z], y, p)) for z, y, p in cells]
    back = [(b, a) for a, b in ring]
    flip_x = [(flat(z, y, p), flat(z, y, p ^ 2)) for z, y, p in cells]
    flip_y = [(flat(z, y, p), flat(z, 1 - y, p)) for z, y, p in cells]
    flip_xy = [(flat(z, y, p), flat(z, 1 - y, p ^ 2)) for z, y, p in cells]
    flip_core = [(flat(z, y, p), flat(z, y, p ^ 1)) for z, y, p in cells]
    return depth, ring, back, (flip_x, flip_y, flip_xy), flip_core


def slot_codes(spot, per_node, capacity):
    rank = lax.broadcasted_iota(jnp.int32, (8 * capacity, 1), 0)
    flip, slot = rank // capacity, rank % capacity
    reach = flip // 4 * per_node + flip % 4
    return ((spot[0] + (spot[1] ^ reach)) * capacity + slot).astype(F32)


def pick_rows(meta, codes, tok, grad, top, outs, pick_ref):
    tok_dev, width = tok.shape
    hit = None
    gate = jnp.zeros(codes.shape, F32)
    for k in range(top):
        same = meta[k : k + 1, :tok_dev] == codes
        value = meta[top + k : top + k + 1, :tok_dev] * 256.0 + meta[2 * top + k : 2 * top + k + 1, :tok_dev]
        gate = gate + jnp.sum(jnp.where(same, value, 0.0), axis=1, keepdims=True)
        hit = same if hit is None else hit | same
    pick = jnp.where(hit, 1.0, 0.0).astype(BF16)
    pick_ref[...] = pick
    scale = gate * (1.0 / 65536.0)
    pair = codes.shape[0] // 4
    for c in range(0, width, COLUMNS):
        cols = slice(c, min(c + COLUMNS, width))
        x = jnp.dot(pick, tok[:, cols], preferred_element_type=F32).astype(BF16)
        dy = (jnp.dot(pick, grad[:, cols], preferred_element_type=F32) * scale).astype(BF16)
        for i, (out_x, out_dy) in enumerate(outs):
            out_x[:, cols] = x[i * pair : (i + 1) * pair]
            out_dy[:, cols] = dy[i * pair : (i + 1) * pair]


def first_kernel(per_node, capacity, experts, spot, *refs):
    far, (*outs, pick_ref, held, codes_ref) = refs[:5], refs[5:12]
    (lists, local, gate, tok, grad), meta, sems = refs[12:17], refs[17], refs[18]
    copies = [pltpu.make_async_copy(a, b, sems.at[i]) for i, (a, b) in enumerate(zip(far, refs[12:17]))]
    for copy in copies:
        copy.start()
    for copy in copies[:3]:
        copy.wait()
    top, tok_dev = local.shape
    width = tok.shape[1]
    place = local[...] // per_node
    group = jnp.zeros_like(place)
    for j in range(lists.shape[0]):
        group = jnp.where(place == j, lists[j : j + 1, :], group)
    expert = group * per_node + local[...] % per_node
    ids = lax.broadcasted_iota(jnp.int32, (experts, tok_dev), 0)
    member = None
    for k in range(top):
        same = ids == expert[k : k + 1, :]
        member = same if member is None else member | same
    rows = lax.broadcasted_iota(jnp.int32, (tok_dev, tok_dev), 0)
    cols = lax.broadcasted_iota(jnp.int32, (tok_dev, tok_dev), 1)
    earlier = jnp.where(rows < cols, 1.0, 0.0).astype(BF16)
    before = jnp.dot(jnp.where(member, 1.0, 0.0).astype(BF16), earlier, preferred_element_type=F32)
    meta[...] = jnp.zeros(meta.shape, F32)
    for k in range(top):
        slot = jnp.sum(jnp.where(ids == expert[k : k + 1, :], before, 0.0), axis=0, keepdims=True)
        code = expert[k : k + 1, :].astype(F32) * capacity + slot
        meta[k : k + 1, :tok_dev] = jnp.where(slot < capacity, code, -1.0)
    meta[top : 2 * top, :tok_dev] = (gate[...] // 256).astype(F32)
    meta[2 * top : 3 * top, :tok_dev] = (gate[...] % 256).astype(F32)
    for copy in copies[3:]:
        copy.wait()
    held[:, :width] = tok[...]
    held[:, width : 2 * width] = grad[...]
    held[:, 2 * width :] = meta[...].astype(BF16)
    codes = slot_codes(spot, per_node, capacity)
    codes_ref[...] = codes
    pick_rows(meta, codes, tok, grad, top, [(out.at[0], out.at[1]) for out in outs], pick_ref)


def next_kernel(top, codes, held, *refs):
    *outs, pick_ref = refs
    width = outs[0].shape[-1]
    meta = held[:, 2 * width :].astype(F32)
    tok, grad = held.at[:, :width], held.at[:, width : 2 * width]
    pairs = list(zip(outs[:4], outs[4:])) if len(outs) == 8 else [(out.at[0], out.at[1]) for out in outs]
    pick_rows(meta, codes[...], tok, grad, top, pairs, pick_ref)


def whole(n):
    return [pl.BlockSpec(memory_space=pltpu.VMEM)] * n


def row_shapes(capacity, tok_dev, width, apart=False):
    shape = (2 * capacity, width)
    rows = [jax.ShapeDtypeStruct(shape, BF16)] * 8 if apart else [jax.ShapeDtypeStruct((2,) + shape, BF16)] * 4
    return rows + [jax.ShapeDtypeStruct((8 * capacity, tok_dev), BF16)]


PARAMS = pltpu.CompilerParams(vmem_limit_bytes=12 * 1024 * 1024)


def first_rows(per_node, capacity, experts, spot, lists, local, gate, tok, grad):
    shape = (tok.shape[0], 2 * tok.shape[1] + META)
    operands = [pltpu.with_memory_space_constraint(a, pltpu.HBM) for a in (lists, local, gate, tok, grad)]
    extra = [jax.ShapeDtypeStruct(shape, BF16), jax.ShapeDtypeStruct((8 * capacity, 1), F32)]
    return pl.pallas_call(
        functools.partial(first_kernel, per_node, capacity, experts),
        in_specs=[pl.BlockSpec(memory_space=pltpu.SMEM)] + [pl.BlockSpec(memory_space=pltpu.HBM)] * 5,
        out_specs=whole(7),
        out_shape=row_shapes(capacity, *tok.shape) + extra,
        scratch_shapes=[pltpu.VMEM(a.shape, a.dtype) for a in (lists, local, gate, tok, grad)]
        + [pltpu.VMEM((tok.shape[0], META), F32), pltpu.SemaphoreType.DMA((5,))],
        compiler_params=PARAMS,
        name="first_rows",
    )(spot, *operands)


def next_rows(top, codes, held, apart):
    shapes = row_shapes(codes.shape[0] // 8, held.shape[0], (held.shape[1] - META) // 2, apart)
    return pl.pallas_call(
        functools.partial(next_kernel, top),
        in_specs=whole(2),
        out_specs=whole(len(shapes)),
        out_shape=shapes,
        compiler_params=PARAMS,
        name="next_rows",
    )(codes, held)


def products(x_rows, w_gate_e, w_up_e):
    gate_act = jnp.dot(x_rows, w_gate_e, preferred_element_type=F32)
    up_act = jnp.dot(x_rows, w_up_e, preferred_element_type=F32)
    return gate_act, up_act


def gradients(gate_act, up_act, dy_rows, w_gate_e, w_up_e, w_down_e):
    last = (((1,), (1,)), ((), ()))
    sig = jax.nn.sigmoid(gate_act)
    hidden = (gate_act * sig * up_act).astype(BF16)
    hidden_grad = lax.dot_general(dy_rows, w_down_e, last, preferred_element_type=F32)
    gate_grad = (hidden_grad * up_act * sig * (1.0 + gate_act * (1.0 - sig))).astype(BF16)
    up_grad = (hidden_grad * gate_act * sig).astype(BF16)
    row_grad = (
        lax.dot_general(gate_grad, w_gate_e, last, preferred_element_type=F32)
        + lax.dot_general(up_grad, w_up_e, last, preferred_element_type=F32)
    ).astype(BF16)
    return hidden, row_grad


def ordered(held, got, w):
    near, far = got[w - 1][1:NEAR], got[w - 2][NEAR:] if w > 1 else []
    held, near, far = lax.optimization_barrier((held, near, far))
    got[w - 1][1:NEAR] = near
    if far:
        got[w - 2][NEAR:] = far
    return held


def body(
    tokens, out_grad, node_lists, expert_local, gate_fixed, gate_weight, up_weight, down_weight
):
    nodes, per_node = lax.axis_size("node"), lax.axis_size("local")
    experts = nodes * per_node
    tok_dev, top = expert_local.shape
    width = tokens.shape[1]
    capacity = tok_dev * top // experts
    depth, ring, back, flips, flip_core = device_perms(nodes, per_node)

    node, place = lax.axis_index("node"), lax.axis_index("local")
    spot = jnp.stack([node // 2 * 2 * per_node, (node % 2) * per_node + place])

    flips_back = [flips[i] for i in (0, 2, 1)]
    picks, got = [], []
    for w in range(depth - 1):
        if w == 0:
            *chosen, pick, held, codes = first_rows(
                per_node, capacity, experts, spot, node_lists.T, expert_local.T, gate_fixed.T, tokens, out_grad
            )
        else:
            ready = ordered(held, got, w)
            held = ready
            *chosen, pick = next_rows(top, codes, ready, False)
        picks.append(pick)
        got.append([chosen[0]] + [lax.ppermute(chosen[i + 1], AXES, flips[i]) for i in (0, 2, 1)])
        held = lax.ppermute(held, AXES, ring)
    *chosen, pick = next_rows(top, codes, ordered(held, got, depth - 1), True)
    picks.append(pick)
    ends = []
    for part in (chosen[:4], chosen[4:]):
        ends.append([part[0]] + [lax.ppermute(part[i + 1], AXES, flips[i]) for i in (0, 2, 1)])
    most = lax.ppermute(jnp.concatenate([g[:, capacity:] for window in got for g in window], axis=1), AXES, flip_core)

    def gather(i, end):
        rest = lax.ppermute(jnp.concatenate([g[capacity:] for g in end], axis=0), AXES, flip_core)
        own = [g[i, :capacity] for window in got for g in window] + [g[:capacity] for g in end]
        return jnp.concatenate(own + [most[i], rest], axis=0)

    x_rows = gather(0, ends[0])
    gate_act, up_act = products(x_rows, gate_weight[0], up_weight[0])
    gate_act, up_act, ends[1] = lax.optimization_barrier((gate_act, up_act, ends[1]))
    dy_rows = gather(1, ends[1])
    hidden, row_grad = gradients(gate_act, up_act, dy_rows, gate_weight[0], up_weight[0], down_weight[0])

    half = depth * 4 * capacity
    own = row_grad[:half].reshape(depth, 4, capacity, width)
    theirs = row_grad[half:].reshape(depth, 4, capacity, width)
    cut = depth // 2
    swapped = [lax.ppermute(theirs[:cut], AXES, flip_core), lax.ppermute(theirs[cut:], AXES, flip_core)]
    swapped = [swapped[w // cut][w % cut] for w in range(depth)]
    BACKPOS = (0, 2, 1)
    groups = [[2], [3], [1], [0]]
    came = {}
    tied = {}
    for group in groups:
        both = jnp.concatenate(
            [jnp.concatenate([own[w], swapped[w]], axis=1).reshape(4, 2 * capacity, width) for w in group], axis=1
        )
        tied[group[0]] = [lax.ppermute(both[i + 1], AXES, flips_back[i]) for i in (0, 2, 1)]
        for n, w in enumerate(group):
            came[w] = (group[0], n, both[0])
    total = None
    sums = {}
    down_local = None
    ahead = depth // 2
    for w in [w for group in groups for w in group]:
        lead, n, mine = came[w]
        pair = 2 * capacity
        parts = [mine[n * pair : (n + 1) * pair]] + [None] * 3
        for i, t in zip((0, 2, 1), tied[lead]):
            parts[BACKPOS[i] + 1] = t[n * pair : (n + 1) * pair]
        total = lax.dot_general(
            picks[w], jnp.concatenate(parts, axis=0), (((0,), (0,)), ((), ())), preferred_element_type=F32
        )
        for extra in sums.get(w, []):
            total = total + extra.astype(F32)
        total = total.astype(BF16)
        if w == 2:
            total, hidden = lax.optimization_barrier((total, hidden))
            down_local = lax.dot_general(
                hidden, dy_rows, (((0,), (0,)), ((), ())), preferred_element_type=F32
            ).astype(BF16)
        if w == 0:
            total, down_local = lax.optimization_barrier((total, down_local))
        if w == 2:
            total, tied[3][:1] = lax.optimization_barrier((total, tied[3][:1]))
        if w:
            dest, perm = (w - 1, back) if w <= ahead else ((w + 1) % depth, ring)
            sums.setdefault(dest, []).append(lax.ppermute(total, AXES, perm))
    return total, down_local[None]


def solution(mesh):
    split = P(AXES)
    return jax.shard_map(
        body, mesh=mesh, in_specs=(split,) * 8, out_specs=(split, split), check_vma=False
    )
```

```python
import functools

import jax
import jax.numpy as jnp
from jax import lax
from jax.experimental import pallas as pl
from jax.experimental.pallas import tpu as pltpu
from jax.sharding import PartitionSpec as P

AXES = ("node", "local")
BF16 = jnp.bfloat16
F32 = jnp.float32
COLUMNS = 1024
META = 128
NEAR = 2


def device_perms(nodes, per_node):
    depth = nodes // 2
    order = [z for z in range(depth) if z == 0 or z % 2 == 1]
    order += [z for z in reversed(range(depth)) if z not in order]
    follow = {order[i]: order[(i + 1) % depth] for i in range(depth)}

    def flat(z, y, place):
        return (z * 2 + y) * per_node + place

    cells = [(z, y, p) for z in range(depth) for y in range(2) for p in range(per_node)]
    ring = [(flat(z, y, p), flat(follow[z], y, p)) for z, y, p in cells]
    back = [(b, a) for a, b in ring]
    flip_x = [(flat(z, y, p), flat(z, y, p ^ 2)) for z, y, p in cells]
    flip_y = [(flat(z, y, p), flat(z, 1 - y, p)) for z, y, p in cells]
    flip_xy = [(flat(z, y, p), flat(z, 1 - y, p ^ 2)) for z, y, p in cells]
    flip_core = [(flat(z, y, p), flat(z, y, p ^ 1)) for z, y, p in cells]
    return depth, ring, back, (flip_x, flip_y, flip_xy), flip_core


def slot_codes(spot, per_node, capacity):
    rank = lax.broadcasted_iota(jnp.int32, (8 * capacity, 1), 0)
    flip, slot = rank // capacity, rank % capacity
    reach = flip // 4 * per_node + flip % 4
    return ((spot[0] + (spot[1] ^ reach)) * capacity + slot).astype(F32)


def pick_rows(meta, codes, tok, grad, top, outs, pick_ref):
    tok_dev, width = tok.shape
    hit = None
    gate = jnp.zeros(codes.shape, F32)
    for k in range(top):
        same = meta[k : k + 1, :tok_dev] == codes
        value = meta[top + k : top + k + 1, :tok_dev] * 256.0 + meta[2 * top + k : 2 * top + k + 1, :tok_dev]
        gate = gate + jnp.sum(jnp.where(same, value, 0.0), axis=1, keepdims=True)
        hit = same if hit is None else hit | same
    pick = jnp.where(hit, 1.0, 0.0).astype(BF16)
    pick_ref[...] = pick
    scale = gate * (1.0 / 65536.0)
    pair = codes.shape[0] // 4
    for c in range(0, width, COLUMNS):
        cols = slice(c, min(c + COLUMNS, width))
        x = jnp.dot(pick, tok[:, cols], preferred_element_type=F32).astype(BF16)
        dy = (jnp.dot(pick, grad[:, cols], preferred_element_type=F32) * scale).astype(BF16)
        for i, (out_x, out_dy) in enumerate(outs):
            out_x[:, cols] = x[i * pair : (i + 1) * pair]
            out_dy[:, cols] = dy[i * pair : (i + 1) * pair]


def first_kernel(per_node, capacity, experts, spot, *refs):
    far, (*outs, pick_ref, held, codes_ref) = refs[:5], refs[5:12]
    (lists, local, gate, tok, grad), meta, sems = refs[12:17], refs[17], refs[18]
    copies = [pltpu.make_async_copy(a, b, sems.at[i]) for i, (a, b) in enumerate(zip(far, refs[12:17]))]
    for copy in copies:
        copy.start()
    for copy in copies[:3]:
        copy.wait()
    top, tok_dev = local.shape
    width = tok.shape[1]
    place = local[...] // per_node
    group = jnp.zeros_like(place)
    for j in range(lists.shape[0]):
        group = jnp.where(place == j, lists[j : j + 1, :], group)
    expert = group * per_node + local[...] % per_node
    ids = lax.broadcasted_iota(jnp.int32, (experts, tok_dev), 0)
    member = None
    for k in range(top):
        same = ids == expert[k : k + 1, :]
        member = same if member is None else member | same
    rows = lax.broadcasted_iota(jnp.int32, (tok_dev, tok_dev), 0)
    cols = lax.broadcasted_iota(jnp.int32, (tok_dev, tok_dev), 1)
    earlier = jnp.where(rows < cols, 1.0, 0.0).astype(BF16)
    before = jnp.dot(jnp.where(member, 1.0, 0.0).astype(BF16), earlier, preferred_element_type=F32)
    meta[...] = jnp.zeros(meta.shape, F32)
    for k in range(top):
        slot = jnp.sum(jnp.where(ids == expert[k : k + 1, :], before, 0.0), axis=0, keepdims=True)
        code = expert[k : k + 1, :].astype(F32) * capacity + slot
        meta[k : k + 1, :tok_dev] = jnp.where(slot < capacity, code, -1.0)
    meta[top : 2 * top, :tok_dev] = (gate[...] // 256).astype(F32)
    meta[2 * top : 3 * top, :tok_dev] = (gate[...] % 256).astype(F32)
    for copy in copies[3:]:
        copy.wait()
    held[:, :width] = tok[...]
    held[:, width : 2 * width] = grad[...]
    held[:, 2 * width :] = meta[...].astype(BF16)
    codes = slot_codes(spot, per_node, capacity)
    codes_ref[...] = codes
    pick_rows(meta, codes, tok, grad, top, [(out.at[0], out.at[1]) for out in outs], pick_ref)


def next_kernel(top, codes, held, *refs):
    *outs, pick_ref = refs
    width = outs[0].shape[-1]
    meta = held[:, 2 * width :].astype(F32)
    tok, grad = held.at[:, :width], held.at[:, width : 2 * width]
    pairs = list(zip(outs[:4], outs[4:])) if len(outs) == 8 else [(out.at[0], out.at[1]) for out in outs]
    pick_rows(meta, codes[...], tok, grad, top, pairs, pick_ref)


def whole(n):
    return [pl.BlockSpec(memory_space=pltpu.VMEM)] * n


def row_shapes(capacity, tok_dev, width, apart=False):
    shape = (2 * capacity, width)
    rows = [jax.ShapeDtypeStruct(shape, BF16)] * 8 if apart else [jax.ShapeDtypeStruct((2,) + shape, BF16)] * 4
    return rows + [jax.ShapeDtypeStruct((8 * capacity, tok_dev), BF16)]


PARAMS = pltpu.CompilerParams(vmem_limit_bytes=12 * 1024 * 1024)


def first_rows(per_node, capacity, experts, spot, lists, local, gate, tok, grad):
    shape = (tok.shape[0], 2 * tok.shape[1] + META)
    operands = [pltpu.with_memory_space_constraint(a, pltpu.HBM) for a in (lists, local, gate, tok, grad)]
    extra = [jax.ShapeDtypeStruct(shape, BF16), jax.ShapeDtypeStruct((8 * capacity, 1), F32)]
    return pl.pallas_call(
        functools.partial(first_kernel, per_node, capacity, experts),
        in_specs=[pl.BlockSpec(memory_space=pltpu.SMEM)] + [pl.BlockSpec(memory_space=pltpu.HBM)] * 5,
        out_specs=whole(7),
        out_shape=row_shapes(capacity, *tok.shape) + extra,
        scratch_shapes=[pltpu.VMEM(a.shape, a.dtype) for a in (lists, local, gate, tok, grad)]
        + [pltpu.VMEM((tok.shape[0], META), F32), pltpu.SemaphoreType.DMA((5,))],
        compiler_params=PARAMS,
        name="first_rows",
    )(spot, *operands)


def next_rows(top, codes, held, apart):
    shapes = row_shapes(codes.shape[0] // 8, held.shape[0], (held.shape[1] - META) // 2, apart)
    return pl.pallas_call(
        functools.partial(next_kernel, top),
        in_specs=whole(2),
        out_specs=whole(len(shapes)),
        out_shape=shapes,
        compiler_params=PARAMS,
        name="next_rows",
    )(codes, held)


def products(x_rows, w_gate_e, w_up_e):
    gate_act = jnp.dot(x_rows, w_gate_e, preferred_element_type=F32)
    up_act = jnp.dot(x_rows, w_up_e, preferred_element_type=F32)
    return gate_act, up_act


def gradients(gate_act, up_act, dy_rows, w_gate_e, w_up_e, w_down_e):
    last = (((1,), (1,)), ((), ()))
    sig = jax.nn.sigmoid(gate_act)
    hidden = (gate_act * sig * up_act).astype(BF16)
    hidden_grad = lax.dot_general(dy_rows, w_down_e, last, preferred_element_type=F32)
    gate_grad = (hidden_grad * up_act * sig * (1.0 + gate_act * (1.0 - sig))).astype(BF16)
    up_grad = (hidden_grad * gate_act * sig).astype(BF16)
    row_grad = (
        lax.dot_general(gate_grad, w_gate_e, last, preferred_element_type=F32)
        + lax.dot_general(up_grad, w_up_e, last, preferred_element_type=F32)
    ).astype(BF16)
    return hidden, row_grad


def turn(rows, flips):
    return [rows[0]] + [lax.ppermute(rows[i + 1], AXES, flips[i]) for i in (0, 2, 1)]


def ordered(held, got, w):
    near, far = got[w - 1][1:NEAR], got[w - 2][NEAR:] if w > 1 else []
    held, near, far = lax.optimization_barrier((held, near, far))
    got[w - 1][1:NEAR] = near
    if far:
        got[w - 2][NEAR:] = far
    return held


def body(
    tokens, out_grad, node_lists, expert_local, gate_fixed, gate_weight, up_weight, down_weight
):
    nodes, per_node = lax.axis_size("node"), lax.axis_size("local")
    experts = nodes * per_node
    tok_dev, top = expert_local.shape
    width = tokens.shape[1]
    capacity = tok_dev * top // experts
    depth, ring, back, flips, flip_core = device_perms(nodes, per_node)

    node, place = lax.axis_index("node"), lax.axis_index("local")
    spot = jnp.stack([node // 2 * 2 * per_node, (node % 2) * per_node + place])

    flips_back = [flips[i] for i in (0, 2, 1)]
    picks, got = [], []
    for w in range(depth - 1):
        if w == 0:
            *chosen, pick, held, codes = first_rows(
                per_node, capacity, experts, spot, node_lists.T, expert_local.T, gate_fixed.T, tokens, out_grad
            )
        else:
            held = ordered(held, got, w)
            *chosen, pick = next_rows(top, codes, held, False)
        picks.append(pick)
        got.append(turn(chosen, flips))
        held = lax.ppermute(held, AXES, ring)
    *chosen, pick = next_rows(top, codes, ordered(held, got, depth - 1), True)
    picks.append(pick)
    ends = [turn(part, flips) for part in (chosen[:4], chosen[4:])]
    most = lax.ppermute(jnp.concatenate([g[:, capacity:] for window in got for g in window], axis=1), AXES, flip_core)

    def gather(i, end):
        rest = lax.ppermute(jnp.concatenate([g[capacity:] for g in end], axis=0), AXES, flip_core)
        own = [g[i, :capacity] for window in got for g in window] + [g[:capacity] for g in end]
        return jnp.concatenate(own + [most[i], rest], axis=0)

    x_rows = gather(0, ends[0])
    gate_act, up_act = products(x_rows, gate_weight[0], up_weight[0])
    gate_act, up_act, ends[1] = lax.optimization_barrier((gate_act, up_act, ends[1]))
    dy_rows = gather(1, ends[1])
    hidden, row_grad = gradients(gate_act, up_act, dy_rows, gate_weight[0], up_weight[0], down_weight[0])

    ahead, order = depth // 2, []
    for i in range(ahead):
        order += [ahead - i] + ([ahead + 1 + i] if ahead + 1 + i < depth else [])
    order.append(0)
    half = depth * 4 * capacity
    own = row_grad[:half].reshape(depth, 4, capacity, width)
    theirs = row_grad[half:].reshape(depth, 4, capacity, width)
    cut = depth // 2
    swapped = [lax.ppermute(theirs[:cut], AXES, flip_core), lax.ppermute(theirs[cut:], AXES, flip_core)]
    swapped = [swapped[w // cut][w % cut] for w in range(depth)]
    mine, sent = {}, {}
    for w in order:
        both = jnp.concatenate([own[w], swapped[w]], axis=1)
        mine[w] = both[0]
        sent[w] = [lax.ppermute(both[n], AXES, flip) for n, flip in ((1, flips[0]), (3, flips[1]), (2, flips[2]))]
    sums = {w: [] for w in order}
    for w in order:
        from_x, from_y, from_xy = sent[w]
        rows = jnp.concatenate([mine[w], from_x, from_y, from_xy], axis=0)
        total = lax.dot_general(picks[w], rows, (((0,), (0,)), ((), ())), preferred_element_type=F32)
        for part in sums[w]:
            total = total + part.astype(F32)
        total = total.astype(BF16)
        if w == order[0]:
            total, hidden = lax.optimization_barrier((total, hidden))
            down_local = lax.dot_general(
                hidden, dy_rows, (((0,), (0,)), ((), ())), preferred_element_type=F32
            ).astype(BF16)
            total, sent[order[1]][:1] = lax.optimization_barrier((total, sent[order[1]][:1]))
        if w == 0:
            total, down_local = lax.optimization_barrier((total, down_local))
        if w:
            dest, perm = (w - 1, back) if w <= ahead else ((w + 1) % depth, ring)
            sums[dest].append(lax.ppermute(total, AXES, perm))
    return total, down_local[None]


def solution(mesh):
    split = P(AXES)
    return jax.shard_map(
        body, mesh=mesh, in_specs=(split,) * 8, out_specs=(split, split), check_vma=False
    )
```

```python
import functools

import jax
import jax.numpy as jnp
from jax import lax
from jax.experimental import pallas as pl
from jax.experimental.pallas import tpu as pltpu
from jax.sharding import PartitionSpec as P

AXES = ("node", "local")
BF16 = jnp.bfloat16
F32 = jnp.float32
COLUMNS = 1024
META = 128
NEAR = 2


def device_perms(nodes, per_node):
    depth = nodes // 2
    order = [z for z in range(depth) if z == 0 or z % 2 == 1]
    order += [z for z in reversed(range(depth)) if z not in order]
    follow = {order[i]: order[(i + 1) % depth] for i in range(depth)}

    def flat(z, y, place):
        return (z * 2 + y) * per_node + place

    cells = [(z, y, p) for z in range(depth) for y in range(2) for p in range(per_node)]
    ring = [(flat(z, y, p), flat(follow[z], y, p)) for z, y, p in cells]
    back = [(b, a) for a, b in ring]
    flip_x = [(flat(z, y, p), flat(z, y, p ^ 2)) for z, y, p in cells]
    flip_y = [(flat(z, y, p), flat(z, 1 - y, p)) for z, y, p in cells]
    flip_xy = [(flat(z, y, p), flat(z, 1 - y, p ^ 2)) for z, y, p in cells]
    flip_core = [(flat(z, y, p), flat(z, y, p ^ 1)) for z, y, p in cells]
    return depth, ring, back, (flip_x, flip_y, flip_xy), flip_core


def split_int(value, size):
    if size & (size - 1):
        return value // size, value % size
    return value >> (size.bit_length() - 1), value & (size - 1)


def slot_codes(spot, per_node, capacity):
    rank = lax.broadcasted_iota(jnp.int32, (8 * capacity, 1), 0)
    flip, slot = split_int(rank, capacity)
    side, local = split_int(flip, 4)
    reach = side * per_node + local
    return ((spot[0] + (spot[1] ^ reach)) * capacity + slot).astype(F32)


def pick_rows(meta, codes, tok, grad, top, outs, pick_ref):
    tok_dev, width = tok.shape
    hit = None
    gate = jnp.zeros(codes.shape, F32)
    for k in range(top):
        same = meta[k : k + 1, :tok_dev] == codes
        value = meta[top + k : top + k + 1, :tok_dev] * 256.0 + meta[2 * top + k : 2 * top + k + 1, :tok_dev]
        gate = gate + jnp.sum(jnp.where(same, value, 0.0), axis=1, keepdims=True)
        hit = same if hit is None else hit | same
    pick = jnp.where(hit, 1.0, 0.0).astype(BF16)
    pick_ref[...] = pick
    scale = gate * (1.0 / 65536.0)
    pair = codes.shape[0] // 4
    for c in range(0, width, COLUMNS):
        cols = slice(c, min(c + COLUMNS, width))
        x = jnp.dot(pick, tok[:, cols], preferred_element_type=F32).astype(BF16)
        dy = (jnp.dot(pick, grad[:, cols], preferred_element_type=F32) * scale).astype(BF16)
        for i, (out_x, out_dy) in enumerate(outs):
            out_x[:, cols] = x[i * pair : (i + 1) * pair]
            out_dy[:, cols] = dy[i * pair : (i + 1) * pair]


def first_kernel(per_node, capacity, experts, spot, *refs):
    far, (*outs, pick_ref, held, codes_ref) = refs[:5], refs[5:12]
    (lists, local, gate), meta, sems = refs[12:15], refs[15], refs[16]
    width = far[3].shape[1]
    tok, grad = held.at[:, :width], held.at[:, width : 2 * width]
    copies = [pltpu.make_async_copy(a, b, sems.at[i]) for i, (a, b) in enumerate(zip(far, (lists, local, gate, tok, grad)))]
    for copy in copies:
        copy.start()
    for copy in copies[:3]:
        copy.wait()
    top, tok_dev = local.shape
    place, member_of = split_int(local[...], per_node)
    group = jnp.zeros_like(place)
    for j in range(lists.shape[0]):
        group = jnp.where(place == j, lists[j : j + 1, :], group)
    expert = group * per_node + member_of
    ids = lax.broadcasted_iota(jnp.int32, (experts, tok_dev), 0)
    member = None
    for k in range(top):
        same = ids == expert[k : k + 1, :]
        member = same if member is None else member | same
    rows = lax.broadcasted_iota(jnp.int32, (tok_dev, tok_dev), 0)
    cols = lax.broadcasted_iota(jnp.int32, (tok_dev, tok_dev), 1)
    earlier = jnp.where(rows < cols, 1.0, 0.0).astype(BF16)
    before = jnp.dot(jnp.where(member, 1.0, 0.0).astype(BF16), earlier, preferred_element_type=F32)
    meta[...] = jnp.zeros(meta.shape, F32)
    for k in range(top):
        slot = jnp.sum(jnp.where(ids == expert[k : k + 1, :], before, 0.0), axis=0, keepdims=True)
        code = expert[k : k + 1, :].astype(F32) * capacity + slot
        meta[k : k + 1, :tok_dev] = jnp.where(slot < capacity, code, -1.0)
    high, low = split_int(gate[...], 256)
    meta[top : 2 * top, :tok_dev] = high.astype(F32)
    meta[2 * top : 3 * top, :tok_dev] = low.astype(F32)
    for copy in copies[3:]:
        copy.wait()
    held[:, 2 * width :] = meta[...].astype(BF16)
    codes = slot_codes(spot, per_node, capacity)
    codes_ref[...] = codes
    pick_rows(meta, codes, tok, grad, top, [(out.at[0], out.at[1]) for out in outs], pick_ref)


def next_kernel(top, codes, held, *refs):
    *outs, pick_ref = refs
    width = outs[0].shape[-1]
    meta = held[:, 2 * width :].astype(F32)
    tok, grad = held.at[:, :width], held.at[:, width : 2 * width]
    pairs = list(zip(outs[:4], outs[4:])) if len(outs) == 8 else [(out.at[0], out.at[1]) for out in outs]
    pick_rows(meta, codes[...], tok, grad, top, pairs, pick_ref)


def whole(n):
    return [pl.BlockSpec(memory_space=pltpu.VMEM)] * n


def row_shapes(capacity, tok_dev, width, apart=False):
    shape = (2 * capacity, width)
    rows = [jax.ShapeDtypeStruct(shape, BF16)] * 8 if apart else [jax.ShapeDtypeStruct((2,) + shape, BF16)] * 4
    return rows + [jax.ShapeDtypeStruct((8 * capacity, tok_dev), BF16)]


PARAMS = pltpu.CompilerParams(vmem_limit_bytes=12 * 1024 * 1024)


def first_rows(per_node, capacity, experts, spot, lists, local, gate, tok, grad):
    shape = (tok.shape[0], 2 * tok.shape[1] + META)
    operands = [pltpu.with_memory_space_constraint(a, pltpu.HBM) for a in (lists, local, gate, tok, grad)]
    extra = [jax.ShapeDtypeStruct(shape, BF16), jax.ShapeDtypeStruct((8 * capacity, 1), F32)]
    return pl.pallas_call(
        functools.partial(first_kernel, per_node, capacity, experts),
        in_specs=[pl.BlockSpec(memory_space=pltpu.SMEM)] + [pl.BlockSpec(memory_space=pltpu.HBM)] * 5,
        out_specs=whole(7),
        out_shape=row_shapes(capacity, *tok.shape) + extra,
        scratch_shapes=[pltpu.VMEM(a.shape, a.dtype) for a in (lists, local, gate)]
        + [pltpu.VMEM((tok.shape[0], META), F32), pltpu.SemaphoreType.DMA((5,))],
        compiler_params=PARAMS,
        name="first_rows",
    )(spot, *operands)


def next_rows(top, codes, held, apart):
    shapes = row_shapes(codes.shape[0] // 8, held.shape[0], (held.shape[1] - META) // 2, apart)
    return pl.pallas_call(
        functools.partial(next_kernel, top),
        in_specs=whole(2),
        out_specs=whole(len(shapes)),
        out_shape=shapes,
        compiler_params=PARAMS,
        name="next_rows",
    )(codes, held)


def products(x_rows, w_gate_e, w_up_e):
    gate_act = jnp.dot(x_rows, w_gate_e, preferred_element_type=F32)
    up_act = jnp.dot(x_rows, w_up_e, preferred_element_type=F32)
    return gate_act, up_act


def gradients(gate_act, up_act, dy_rows, w_gate_e, w_up_e, w_down_e):
    last = (((1,), (1,)), ((), ()))
    sig = jax.nn.sigmoid(gate_act)
    hidden = (gate_act * sig * up_act).astype(BF16)
    hidden_grad = lax.dot_general(dy_rows, w_down_e, last, preferred_element_type=F32)
    gate_grad = (hidden_grad * up_act * sig * (1.0 + gate_act * (1.0 - sig))).astype(BF16)
    up_grad = (hidden_grad * gate_act * sig).astype(BF16)
    row_grad = (
        lax.dot_general(gate_grad, w_gate_e, last, preferred_element_type=F32)
        + lax.dot_general(up_grad, w_up_e, last, preferred_element_type=F32)
    ).astype(BF16)
    return hidden, row_grad


def turn(rows, flips):
    return [rows[0]] + [lax.ppermute(rows[i + 1], AXES, flips[i]) for i in (0, 2, 1)]


def ordered(held, got, w):
    near, far = got[w - 1][1:NEAR], got[w - 2][NEAR:] if w > 1 else []
    held, near, far = lax.optimization_barrier((held, near, far))
    got[w - 1][1:NEAR] = near
    if far:
        got[w - 2][NEAR:] = far
    return held


def body(
    tokens, out_grad, node_lists, expert_local, gate_fixed, gate_weight, up_weight, down_weight
):
    nodes, per_node = lax.axis_size("node"), lax.axis_size("local")
    experts = nodes * per_node
    tok_dev, top = expert_local.shape
    width = tokens.shape[1]
    capacity = tok_dev * top // experts
    depth, ring, back, flips, flip_core = device_perms(nodes, per_node)

    node, place = lax.axis_index("node"), lax.axis_index("local")
    spot = jnp.stack([node // 2 * 2 * per_node, (node % 2) * per_node + place])

    picks, got = [], []
    for w in range(depth - 1):
        if w == 0:
            *chosen, pick, held, codes = first_rows(
                per_node, capacity, experts, spot, node_lists.T, expert_local.T, gate_fixed.T, tokens, out_grad
            )
        else:
            held = ordered(held, got, w)
            *chosen, pick = next_rows(top, codes, held, False)
        picks.append(pick)
        after = lax.ppermute(held, AXES, ring)
        got.append(turn(chosen, flips))
        held = after
    *chosen, pick = next_rows(top, codes, ordered(held, got, depth - 1), True)
    picks.append(pick)
    ends = [turn(part, flips) for part in (chosen[:4], chosen[4:])]
    most = lax.ppermute(jnp.concatenate([g[:, capacity:] for window in got for g in window], axis=1), AXES, flip_core)

    def gather(i, end):
        rest = lax.ppermute(jnp.concatenate([g[capacity:] for g in end], axis=0), AXES, flip_core)
        own = [g[i, :capacity] for window in got for g in window] + [g[:capacity] for g in end]
        return jnp.concatenate(own + [most[i], rest], axis=0)

    x_rows = gather(0, ends[0])
    gate_act, up_act = products(x_rows, gate_weight[0], up_weight[0])
    gate_act, up_act, ends[1] = lax.optimization_barrier((gate_act, up_act, ends[1]))
    dy_rows = gather(1, ends[1])
    hidden, row_grad = gradients(gate_act, up_act, dy_rows, gate_weight[0], up_weight[0], down_weight[0])

    ahead, order = depth // 2, []
    for i in range(ahead):
        order += [ahead - i] + ([ahead + 1 + i] if ahead + 1 + i < depth else [])
    order.append(0)
    half = depth * 4 * capacity
    own = row_grad[:half].reshape(depth, 4, capacity, width)
    theirs = row_grad[half:].reshape(depth, 4, capacity, width)
    cut = depth // 2
    swapped = [lax.ppermute(theirs[:cut], AXES, flip_core), lax.ppermute(theirs[cut:], AXES, flip_core)]
    swapped = [swapped[w // cut][w % cut] for w in range(depth)]
    mine, sent = {}, {}
    for w in order:
        both = jnp.concatenate([own[w], swapped[w]], axis=1)
        mine[w] = both[0]
        sent[w] = [lax.ppermute(both[n], AXES, flip) for n, flip in ((1, flips[0]), (3, flips[1]), (2, flips[2]))]
    sums = {w: [] for w in order}
    for w in order:
        from_x, from_y, from_xy = sent[w]
        rows = jnp.concatenate([mine[w], from_x, from_y, from_xy], axis=0)
        total = lax.dot_general(picks[w], rows, (((0,), (0,)), ((), ())), preferred_element_type=F32)
        for part in sums[w]:
            total = total + part.astype(F32)
        total = total.astype(BF16)
        if w == order[0]:
            total, hidden = lax.optimization_barrier((total, hidden))
            down_local = lax.dot_general(
                hidden, dy_rows, (((0,), (0,)), ((), ())), preferred_element_type=F32
            ).astype(BF16)
            total, sent[order[1]][:1] = lax.optimization_barrier((total, sent[order[1]][:1]))
        if w == 0:
            total, down_local = lax.optimization_barrier((total, down_local))
        if w == order[1]:
            total, sent[order[2]][:1] = lax.optimization_barrier((total, sent[order[2]][:1]))
        if w:
            dest, perm = (w - 1, back) if w <= ahead else ((w + 1) % depth, ring)
            sums[dest].append(lax.ppermute(total, AXES, perm))
    return total, down_local[None]


def solution(mesh):
    split = P(AXES)
    return jax.shard_map(
        body, mesh=mesh, in_specs=(split,) * 8, out_specs=(split, split), check_vma=False
    )
```

```python
import functools

import jax
import jax.numpy as jnp
from jax import lax
from jax.experimental import pallas as pl
from jax.experimental.pallas import tpu as pltpu
from jax.sharding import PartitionSpec as P

AXES = ("node", "local")
BF16 = jnp.bfloat16
F32 = jnp.float32
COLUMNS = 1024
META = 128
NEAR = 1


def device_perms(nodes, per_node):
    depth = nodes // 2
    order = [z for z in range(depth) if z == 0 or z % 2 == 1]
    order += [z for z in reversed(range(depth)) if z not in order]
    follow = {order[i]: order[(i + 1) % depth] for i in range(depth)}

    def flat(z, y, place):
        return (z * 2 + y) * per_node + place

    cells = [(z, y, p) for z in range(depth) for y in range(2) for p in range(per_node)]
    ring = [(flat(z, y, p), flat(follow[z], y, p)) for z, y, p in cells]
    back = [(b, a) for a, b in ring]
    flip_x = [(flat(z, y, p), flat(z, y, p ^ 2)) for z, y, p in cells]
    flip_y = [(flat(z, y, p), flat(z, 1 - y, p)) for z, y, p in cells]
    flip_xy = [(flat(z, y, p), flat(z, 1 - y, p ^ 2)) for z, y, p in cells]
    flip_core = [(flat(z, y, p), flat(z, y, p ^ 1)) for z, y, p in cells]
    return depth, ring, back, (flip_x, flip_y, flip_xy), flip_core


def slot_codes(spot, per_node, capacity):
    rank = lax.broadcasted_iota(jnp.int32, (8 * capacity, 1), 0)
    flip, slot = rank // capacity, rank % capacity
    reach = flip // 4 * per_node + flip % 4
    return ((spot[0] + (spot[1] ^ reach)) * capacity + slot).astype(F32)


def pick_rows(meta, codes, tok, grad, top, outs, pick_ref):
    tok_dev, width = tok.shape
    hit = None
    gate = jnp.zeros(codes.shape, F32)
    for k in range(top):
        same = meta[k : k + 1, :tok_dev] == codes
        value = meta[top + k : top + k + 1, :tok_dev] * 256.0 + meta[2 * top + k : 2 * top + k + 1, :tok_dev]
        gate = gate + jnp.sum(jnp.where(same, value, 0.0), axis=1, keepdims=True)
        hit = same if hit is None else hit | same
    pick = jnp.where(hit, 1.0, 0.0).astype(BF16)
    pick_ref[...] = pick
    scale = gate * (1.0 / 65536.0)
    pair = codes.shape[0] // 4
    for c in range(0, width, COLUMNS):
        cols = slice(c, min(c + COLUMNS, width))
        x = jnp.dot(pick, tok[:, cols], preferred_element_type=F32).astype(BF16)
        dy = (jnp.dot(pick, grad[:, cols], preferred_element_type=F32) * scale).astype(BF16)
        for i, (out_x, out_dy) in enumerate(outs):
            out_x[:, cols] = x[i * pair : (i + 1) * pair]
            out_dy[:, cols] = dy[i * pair : (i + 1) * pair]


def first_kernel(per_node, capacity, experts, spot, *refs):
    far, (*outs, pick_ref, held, codes_ref) = refs[:5], refs[5:12]
    (lists, local, gate, tok, grad), meta, sems = refs[12:17], refs[17], refs[18]
    copies = [pltpu.make_async_copy(a, b, sems.at[i]) for i, (a, b) in enumerate(zip(far, refs[12:17]))]
    for copy in copies:
        copy.start()
    for copy in copies[:3]:
        copy.wait()
    top, tok_dev = local.shape
    width = tok.shape[1]
    place = local[...] // per_node
    group = jnp.zeros_like(place)
    for j in range(lists.shape[0]):
        group = jnp.where(place == j, lists[j : j + 1, :], group)
    expert = group * per_node + local[...] % per_node
    ids = lax.broadcasted_iota(jnp.int32, (experts, tok_dev), 0)
    member = None
    for k in range(top):
        same = ids == expert[k : k + 1, :]
        member = same if member is None else member | same
    rows = lax.broadcasted_iota(jnp.int32, (tok_dev, tok_dev), 0)
    cols = lax.broadcasted_iota(jnp.int32, (tok_dev, tok_dev), 1)
    earlier = jnp.where(rows < cols, 1.0, 0.0).astype(BF16)
    before = jnp.dot(jnp.where(member, 1.0, 0.0).astype(BF16), earlier, preferred_element_type=F32)
    meta[...] = jnp.zeros(meta.shape, F32)
    for k in range(top):
        slot = jnp.sum(jnp.where(ids == expert[k : k + 1, :], before, 0.0), axis=0, keepdims=True)
        code = expert[k : k + 1, :].astype(F32) * capacity + slot
        meta[k : k + 1, :tok_dev] = jnp.where(slot < capacity, code, -1.0)
    meta[top : 2 * top, :tok_dev] = (gate[...] // 256).astype(F32)
    meta[2 * top : 3 * top, :tok_dev] = (gate[...] % 256).astype(F32)
    for copy in copies[3:]:
        copy.wait()
    held[:, :width] = grad[...]
    held[:, width:] = meta[...].astype(BF16)
    codes = slot_codes(spot, per_node, capacity)
    codes_ref[...] = codes
    pick_rows(meta, codes, tok, grad, top, [(out.at[0], out.at[1]) for out in outs], pick_ref)


def next_kernel(top, codes, tok, held, *refs):
    *outs, pick_ref = refs
    width = outs[0].shape[-1]
    meta = held[:, width:].astype(F32)
    grad = held.at[:, :width]
    pairs = list(zip(outs[:4], outs[4:])) if len(outs) == 8 else [(out.at[0], out.at[1]) for out in outs]
    pick_rows(meta, codes[...], tok, grad, top, pairs, pick_ref)


def whole(n):
    return [pl.BlockSpec(memory_space=pltpu.VMEM)] * n


def row_shapes(capacity, tok_dev, width, apart=False):
    shape = (2 * capacity, width)
    rows = [jax.ShapeDtypeStruct(shape, BF16)] * 8 if apart else [jax.ShapeDtypeStruct((2,) + shape, BF16)] * 4
    return rows + [jax.ShapeDtypeStruct((8 * capacity, tok_dev), BF16)]


PARAMS = pltpu.CompilerParams(vmem_limit_bytes=12 * 1024 * 1024)


def first_rows(per_node, capacity, experts, spot, lists, local, gate, tok, grad):
    shape = (tok.shape[0], tok.shape[1] + META)
    operands = [pltpu.with_memory_space_constraint(a, pltpu.HBM) for a in (lists, local, gate, tok, grad)]
    extra = [jax.ShapeDtypeStruct(shape, BF16), jax.ShapeDtypeStruct((8 * capacity, 1), F32)]
    return pl.pallas_call(
        functools.partial(first_kernel, per_node, capacity, experts),
        in_specs=[pl.BlockSpec(memory_space=pltpu.SMEM)] + [pl.BlockSpec(memory_space=pltpu.HBM)] * 5,
        out_specs=whole(7),
        out_shape=row_shapes(capacity, *tok.shape) + extra,
        scratch_shapes=[pltpu.VMEM(a.shape, a.dtype) for a in (lists, local, gate, tok, grad)]
        + [pltpu.VMEM((tok.shape[0], META), F32), pltpu.SemaphoreType.DMA((5,))],
        compiler_params=PARAMS,
        name="first_rows",
    )(spot, *operands)


def next_rows(top, codes, tok, held, apart):
    shapes = row_shapes(codes.shape[0] // 8, *tok.shape, apart)
    return pl.pallas_call(
        functools.partial(next_kernel, top),
        in_specs=whole(3),
        out_specs=whole(len(shapes)),
        out_shape=shapes,
        compiler_params=PARAMS,
        name="next_rows",
    )(codes, tok, held)


def products(x_rows, w_gate_e, w_up_e):
    gate_act = jnp.dot(x_rows, w_gate_e, preferred_element_type=F32)
    up_act = jnp.dot(x_rows, w_up_e, preferred_element_type=F32)
    return gate_act, up_act


def gradients(gate_act, up_act, dy_rows, w_gate_e, w_up_e, w_down_e):
    last = (((1,), (1,)), ((), ()))
    sig = jax.nn.sigmoid(gate_act)
    hidden = (gate_act * sig * up_act).astype(BF16)
    hidden_grad = lax.dot_general(dy_rows, w_down_e, last, preferred_element_type=F32)
    gate_grad = (hidden_grad * up_act * sig * (1.0 + gate_act * (1.0 - sig))).astype(BF16)
    up_grad = (hidden_grad * gate_act * sig).astype(BF16)
    row_grad = (
        lax.dot_general(gate_grad, w_gate_e, last, preferred_element_type=F32)
        + lax.dot_general(up_grad, w_up_e, last, preferred_element_type=F32)
    ).astype(BF16)
    return hidden, row_grad


def turn(rows, flips):
    return [rows[0]] + [lax.ppermute(rows[i + 1], AXES, flips[i]) for i in (0, 2, 1)]


def ordered(held, got, w):
    near, far = got[w - 1][1:NEAR], got[w - 2][NEAR:] if w > 1 else []
    held, near, far = lax.optimization_barrier((held, near, far))
    got[w - 1][1:NEAR] = near
    if far:
        got[w - 2][NEAR:] = far
    return held


def body(
    tokens, out_grad, node_lists, expert_local, gate_fixed, gate_weight, up_weight, down_weight
):
    nodes, per_node = lax.axis_size("node"), lax.axis_size("local")
    experts = nodes * per_node
    tok_dev, top = expert_local.shape
    width = tokens.shape[1]
    capacity = tok_dev * top // experts
    depth, ring, back, flips, flip_core = device_perms(nodes, per_node)

    node, place = lax.axis_index("node"), lax.axis_index("local")
    spot = jnp.stack([node // 2 * 2 * per_node, (node % 2) * per_node + place])

    tok, picks, got = tokens, [], []
    for w in range(depth - 1):
        if w == 0:
            *chosen, pick, held, codes = first_rows(
                per_node, capacity, experts, spot, node_lists.T, expert_local.T, gate_fixed.T, tokens, out_grad
            )
        else:
            held = ordered(held, got, w)
            *chosen, pick = next_rows(top, codes, tok, held, False)
        picks.append(pick)
        got.append(turn(chosen, flips))
        tok, held = lax.ppermute(tok, AXES, ring), lax.ppermute(held, AXES, ring)
    *chosen, pick = next_rows(top, codes, tok, ordered(held, got, depth - 1), True)
    picks.append(pick)
    ends = [turn(part, flips) for part in (chosen[:4], chosen[4:])]
    most = lax.ppermute(jnp.concatenate([g[:, capacity:] for window in got for g in window], axis=1), AXES, flip_core)

    def gather(i, end):
        rest = lax.ppermute(jnp.concatenate([g[capacity:] for g in end], axis=0), AXES, flip_core)
        own = [g[i, :capacity] for window in got for g in window] + [g[:capacity] for g in end]
        return jnp.concatenate(own + [most[i], rest], axis=0)

    x_rows = gather(0, ends[0])
    gate_act, up_act = products(x_rows, gate_weight[0], up_weight[0])
    gate_act, up_act, ends[1] = lax.optimization_barrier((gate_act, up_act, ends[1]))
    dy_rows = gather(1, ends[1])
    hidden, row_grad = gradients(gate_act, up_act, dy_rows, gate_weight[0], up_weight[0], down_weight[0])

    ahead, order = depth // 2, []
    for i in range(ahead):
        order += [ahead - i] + ([ahead + 1 + i] if ahead + 1 + i < depth else [])
    order.append(0)
    half = depth * 4 * capacity
    own = row_grad[:half].reshape(depth, 4, capacity, width)
    theirs = row_grad[half:].reshape(depth, 4, capacity, width)
    cut = depth // 2
    swapped = [lax.ppermute(theirs[:cut], AXES, flip_core), lax.ppermute(theirs[cut:], AXES, flip_core)]
    swapped = [swapped[w // cut][w % cut] for w in range(depth)]
    mine, sent = {}, {}
    for w in order:
        both = jnp.concatenate([own[w], swapped[w]], axis=1)
        mine[w] = both[0]
        sent[w] = [lax.ppermute(both[n], AXES, flip) for n, flip in ((1, flips[0]), (3, flips[1]), (2, flips[2]))]
    sums = {w: [] for w in order}
    for w in order:
        from_x, from_y, from_xy = sent[w]
        rows = jnp.concatenate([mine[w], from_x, from_y, from_xy], axis=0)
        total = lax.dot_general(picks[w], rows, (((0,), (0,)), ((), ())), preferred_element_type=F32)
        for part in sums[w]:
            total = total + part.astype(F32)
        total = total.astype(BF16)
        if w == order[0]:
            total, hidden = lax.optimization_barrier((total, hidden))
            down_local = lax.dot_general(
                hidden, dy_rows, (((0,), (0,)), ((), ())), preferred_element_type=F32
            ).astype(BF16)
            total, sent[order[1]][:1] = lax.optimization_barrier((total, sent[order[1]][:1]))
        if w == 0:
            total, down_local = lax.optimization_barrier((total, down_local))
        if w == order[1]:
            total, sent[order[2]][:1] = lax.optimization_barrier((total, sent[order[2]][:1]))
        if w:
            dest, perm = (w - 1, back) if w <= ahead else ((w + 1) % depth, ring)
            sums[dest].append(lax.ppermute(total, AXES, perm))
    return total, down_local[None]


def solution(mesh):
    split = P(AXES)
    return jax.shard_map(
        body, mesh=mesh, in_specs=(split,) * 8, out_specs=(split, split), check_vma=False
    )
```
